512 devices in a mesh: clip: 32 (over x, z), seq: 8 (over y), tp: 2 (over core).
Axes of the slice: x: 4, y: 8, z: 8, core: 2. Of those that a mesh axis runs over, the one named last changes fastest.
Arguments:
- projections: bfloat16 [65536, 32, 384], P(('clip', 'seq', 'tp')), parts along dimension 0, may hold values from -64 to 64
- tile_mask: int32 [1024, 16, 16], P('clip'), parts along dimension 0, may hold values from 0 to 1, as said below
Outputs:
- attention: bfloat16 [65536, 4096], P(('clip', 'seq', 'tp')), parts along dimension 0
The draws below stay inside these ranges and needn't reach their ends.
There are 32 independent parts, one for each index of `clip`. The reference program is written for one: setup_inputs(seed, part) draws one part's arguments, and reference() takes and returns one part's arrays. A program takes and returns all parts, laid end to end along the dimension named above; each array names one. Nothing has to cross between parts.
Inputs may be any that keep to these rules, and one draw needn't show every extreme that they name: tile_mask[h, a, a] = 1 for every head h and tile a.
All inputs are finite; a program needn't handle non-finite values.
Results may differ from the reference program's by a relative error of at most 0.0055.
Values may be sent and summed in bfloat16 or wider, within the bound.
A program may use at most 64 MiB of HBM per device.

```python
import math
import jax
import jax.numpy as jnp
from jax import lax

H = 32
HDIM = 128
TILE = 128
SPAN = 512
TOKENS = 2048


def draw_projections(key, part):
    key = jax.random.fold_in(key, 11)
    shape = (TOKENS, H, 3 * HDIM)
    base = jnp.clip(jax.random.normal(key, shape, jnp.float32), -6.0, 6.0)
    factors = jnp.concatenate([jnp.full((HDIM,), 2.0, jnp.float32), jnp.ones((2 * HDIM,), jnp.float32)])
    result = base * factors
    return result.astype(jnp.bfloat16)


def draw_tile_mask(key, part):
    key = jax.random.fold_in(key, 23)
    reach_key, column_key = jax.random.split(key)
    tile_count = TOKENS // TILE
    reach = jax.random.randint(reach_key, (H, 1, 1), 1, tile_count + 1)
    columns = jax.random.randint(column_key, (H, 1, tile_count), 0, 8) == 0
    tile_ids = jnp.arange(tile_count)
    band = jnp.abs(tile_ids[:, None] - tile_ids[None, :])[None, :, :] < reach
    return (band | columns).astype(jnp.int32)


def setup_inputs(seed: int = 0, part: int = 0) -> dict:
    arg_keys = jax.random.split(jax.random.key(seed), 3)
    part_splits = jax.random.split(jax.random.fold_in(arg_keys[2], part), 3)
    projections = draw_projections(jax.random.fold_in(jax.random.fold_in(arg_keys[2], part), 71), part)
    tile_mask = draw_tile_mask(jax.random.fold_in(jax.random.fold_in(arg_keys[2], part), 71), part)
    return dict(projections=projections, tile_mask=tile_mask)


NEGATIVE_FILL = -1e+30

def reference(projections, tile_mask):
    seq_length, head_count, row_width = projections.shape
    head_dim = row_width // 3
    score_scale = 1.0 / math.sqrt(head_dim)
    block_count = seq_length // SPAN
    tiles_per_block = SPAN // TILE

    def one_head(head_index):
        head_data = lax.dynamic_index_in_dim(projections, head_index, 1, keepdims=False)
        head_tiles = lax.dynamic_index_in_dim(tile_mask, head_index, 0, keepdims=False)
        key_allowed = jnp.repeat(head_tiles, TILE, axis=1) > 0

        def one_block(block_index):
            start = (block_index * SPAN).astype(jnp.int32)
            queries = lax.dynamic_slice_in_dim(head_data, start, SPAN, 0)[:, :head_dim]
            scores = lax.dot_general(queries, head_data[:, head_dim:2 * head_dim], (((1,), (1,)), ((), ())), preferred_element_type=jnp.float32) * score_scale
            tile_rows = lax.dynamic_slice_in_dim(key_allowed, (block_index * tiles_per_block).astype(jnp.int32), tiles_per_block, 0)
            allowed = jnp.repeat(tile_rows, TILE, axis=0)
            masked = jnp.where(allowed, scores, NEGATIVE_FILL)
            row_max = lax.optimization_barrier(jnp.max(masked, axis=1))
            expo = jnp.where(allowed, jnp.exp(masked - row_max[:, None]), 0.0)
            row_sum = lax.optimization_barrier(jnp.sum(expo, axis=1))
            weights = expo.astype(jnp.bfloat16)
            summed = jnp.dot(weights, head_data[:, 2 * head_dim:], preferred_element_type=jnp.float32)
            return (summed / row_sum[:, None]).astype(jnp.bfloat16)
        outputs = lax.map(one_block, jnp.arange(block_count, dtype=jnp.int32))
        return outputs.reshape(seq_length, head_dim)
    results = lax.map(one_head, jnp.arange(head_count, dtype=jnp.int32))
    return jnp.transpose(results, (1, 0, 2)).reshape(seq_length, head_count * head_dim)
```

```python
import functools
import math

import jax
import jax.numpy as jnp
from jax import lax
from jax.experimental import pallas as pl
from jax.experimental.pallas import tpu as pltpu
from jax.sharding import PartitionSpec as P

MESH = pl.DeviceIdType.MESH
NEGATIVE_FILL = -1e30
CHIPS = 8
CORES = 2
PEERS = CHIPS * CORES
REACH = (1, 7, 2, 6, 3, 5, 4)
OFFSETS = tuple((d, f) for d in REACH for f in range(CORES)) + ((0, 1),)


def kernel(
    x_ref,
    mask_ref,
    out_ref,
    x_in,
    mask_in,
    kv_out,
    q_out,
    kv_got,
    q_got,
    o_out,
    tile_of_key,
    bias,
    scores,
    in_sem,
    mask_sem,
    own_sem,
    send_sem,
    recv_sem,
):
    y = lax.axis_index("seq")
    core = lax.axis_index("tp")
    me = y * CORES + core
    tokens, _, width = x_ref.shape
    slots = x_in.shape[0]
    dim = width // 3
    pair = CORES * tokens
    keys = kv_got.shape[1]

    for slot in range(slots):
        pltpu.make_async_copy(
            x_ref.at[:, pl.ds(slot * PEERS, PEERS), :], x_in.at[slot], in_sem.at[slot]
        ).start()
        pltpu.make_async_copy(
            mask_ref.at[slot * PEERS + me], mask_in.at[slot], mask_sem.at[slot]
        ).start()

    def peer(d, f):
        return {"seq": lax.rem(y + d, CHIPS), "tp": lax.rem(core + f, CORES)}

    def index_of(d, f):
        return lax.rem(y + d, CHIPS) * CORES + lax.rem(core + f, CORES)

    barrier = pltpu.get_barrier_semaphore()
    for d, f in OFFSETS:
        pl.semaphore_signal(barrier, inc=1, device_id=peer(d, f), device_id_type=MESH)

    def rows_of(device):
        return pl.ds(pl.multiple_of(device * tokens, tokens), tokens)

    def remote(kind, slot, d, f):
        to = index_of(d, f)
        if kind == "kv":
            src, dst, row = kv_out.at[slot, to], kv_got.at[slot, rows_of(me)], slot
        elif kind == "q":
            src, dst, row = q_out.at[slot, to], q_got.at[slot, rows_of(me)], 2 + slot
        else:
            columns = pl.ds(pl.multiple_of((slot * PEERS + me) * dim, dim), dim)
            src, dst, row = o_out.at[slot, rows_of(to)], out_ref.at[:, columns], 4 + slot
        number = d * CORES + f
        return pltpu.make_async_remote_copy(
            src_ref=src,
            dst_ref=dst,
            send_sem=send_sem.at[row, number],
            recv_sem=recv_sem.at[row, number],
            device_id=peer(d, f),
            device_id_type=MESH,
        )

    def own(kind, slot):
        if kind == "kv":
            src, dst, row = kv_out.at[slot, me], kv_got.at[slot, rows_of(me)], slot
        elif kind == "q":
            src, dst, row = q_out.at[slot, me], q_got.at[slot, rows_of(me)], 2 + slot
        else:
            columns = pl.ds(pl.multiple_of((slot * PEERS + me) * dim, dim), dim)
            src, dst, row = o_out.at[slot, rows_of(me)], out_ref.at[:, columns], 4 + slot
        return pltpu.make_async_copy(src, dst, own_sem.at[row])

    tile_of_key[...] = (
        lax.broadcasted_iota(jnp.int32, tile_of_key.shape, 0) // tokens
        == lax.broadcasted_iota(jnp.int32, tile_of_key.shape, 1)
    ).astype(jnp.bfloat16)
    bias[...] = jnp.zeros_like(bias)
    for slot in range(slots):
        pltpu.make_async_copy(
            mask_ref.at[slot * PEERS + me], mask_in.at[slot], mask_sem.at[slot]
        ).wait()
        bias[slot, :, 0:PEERS] = jnp.where(mask_in[slot] > 0, 0.0, NEGATIVE_FILL)

    side = PEERS * PEERS
    to_row = lax.broadcasted_iota(jnp.int32, (side, side), 0)
    from_row = lax.broadcasted_iota(jnp.int32, (side, side), 1)
    swap = (from_row == (to_row % PEERS) * PEERS + to_row // PEERS).astype(jnp.bfloat16)

    def regroup(slot, columns, target):
        for start in range(0, tokens, PEERS):
            block = x_in[slot, start : start + PEERS, :, columns].reshape(side, -1)
            swapped = jnp.dot(swap, block, preferred_element_type=jnp.float32)
            target[slot, :, start : start + PEERS, :] = swapped.astype(jnp.bfloat16).reshape(
                PEERS, PEERS, -1
            )

    for slot in range(slots):
        pltpu.make_async_copy(
            x_ref.at[:, pl.ds(slot * PEERS, PEERS), :], x_in.at[slot], in_sem.at[slot]
        ).wait()
        regroup(slot, slice(dim, 3 * dim), kv_out)
        if slot == 0:
            pl.semaphore_wait(barrier, len(OFFSETS))
        for d, f in OFFSETS:
            remote("kv", slot, d, f).start()
        own("kv", slot).start()
        regroup(slot, slice(0, dim), q_out)
        for d, f in OFFSETS:
            remote("q", slot, d, f).start()
        own("q", slot).start()

    exponent_scale = math.log2(math.e) / math.sqrt(dim)
    ones = jnp.ones((2 * dim, dim), jnp.bfloat16)
    step = 2 * dim

    def attend(slot, chip):
        rows = pl.ds(pl.multiple_of(chip * pair, pair), pair)
        biases = jnp.concatenate(
            [
                jnp.broadcast_to(bias[slot, pl.ds(chip * CORES + i, 1), :], (tokens, dim))
                for i in range(CORES)
            ],
            axis=0,
        )
        queries = jnp.concatenate([q_got[slot, rows, :], biases.astype(jnp.bfloat16)], axis=1)
        largest = None
        for start in range(0, keys, step):
            part = slice(start, start + step)
            key_part = jnp.concatenate([kv_got[slot, part, 0:dim], tile_of_key[part, :]], axis=1)
            found = lax.dot_general(
                queries, key_part, (((1,), (1,)), ((), ())), preferred_element_type=jnp.float32
            )
            scores[:, part] = found
            higher = jnp.maximum(found[:, 0:dim], found[:, dim:step])
            largest = higher if largest is None else jnp.maximum(largest, higher)
        row_max = jnp.max(largest, axis=1, keepdims=True)
        total = jnp.zeros((pair, 2 * dim), jnp.float32)
        for start in range(0, keys, step):
            part = slice(start, start + step)
            weights = jnp.exp2((scores[:, part] - row_max) * exponent_scale).astype(jnp.bfloat16)
            values = jnp.concatenate([kv_got[slot, part, dim : 2 * dim], ones], axis=1)
            total += jnp.dot(weights, values, preferred_element_type=jnp.float32)
        o_out[slot, rows, :] = (total[:, 0:dim] / total[:, dim : 2 * dim]).astype(jnp.bfloat16)

    for slot in range(slots):
        with jax.named_scope("wait_kv"):
            own("kv", slot).wait()
            for d, f in OFFSETS:
                remote("kv", slot, d, f).wait_recv()
        own("q", slot).wait()
        remote("q", slot, 0, 1).wait_recv()
        attend(slot, y)
        own("o", slot).start()
        remote("o", slot, 0, 1).start()

        def turn(number, carry, slot=slot):
            distance = (number + 2) // 2
            d = jnp.where(number % 2 == 0, distance, CHIPS - distance)
            for f in range(CORES):
                remote("q", slot, CHIPS - d, f).wait_recv()
            attend(slot, lax.rem(y + d, CHIPS))
            for f in range(CORES):
                remote("o", slot, d, f).start()
            return carry

        with jax.named_scope("attend"):
            lax.fori_loop(0, CHIPS - 1, turn, 0)

    with jax.named_scope("wait_last"):
        for slot in range(slots):
            own("o", slot).wait()
            for d, f in OFFSETS:
                remote("o", slot, d, f).wait_recv()
                for kind in ("kv", "q", "o"):
                    remote(kind, slot, d, f).wait_send()


def body(projections, tile_mask):
    tokens, heads, width = projections.shape
    dim = width // 3
    slots = heads // PEERS
    keys = tokens * PEERS
    return pl.pallas_call(
        kernel,
        out_shape=jax.ShapeDtypeStruct((tokens, heads * dim), jnp.bfloat16),
        in_specs=[pl.BlockSpec(memory_space=pl.ANY)] * 2,
        out_specs=pl.BlockSpec(memory_space=pl.ANY),
        scratch_shapes=[
            pltpu.VMEM((slots, tokens, PEERS, width), jnp.bfloat16),
            pltpu.VMEM((slots, PEERS, PEERS), jnp.int32),
            pltpu.VMEM((slots, PEERS, tokens, 2 * dim), jnp.bfloat16),
            pltpu.VMEM((slots, PEERS, tokens, dim), jnp.bfloat16),
            pltpu.VMEM((slots, keys, 2 * dim), jnp.bfloat16),
            pltpu.VMEM((slots, keys, dim), jnp.bfloat16),
            pltpu.VMEM((slots, keys, dim), jnp.bfloat16),
            pltpu.VMEM((keys, dim), jnp.bfloat16),
            pltpu.VMEM((slots, PEERS, dim), jnp.float32),
            pltpu.VMEM((CORES * tokens, keys), jnp.float32),
            pltpu.SemaphoreType.DMA((slots,)),
            pltpu.SemaphoreType.DMA((slots,)),
            pltpu.SemaphoreType.DMA((3 * slots,)),
            pltpu.SemaphoreType.DMA((3 * slots, PEERS)),
            pltpu.SemaphoreType.DMA((3 * slots, PEERS)),
        ],
        compiler_params=pltpu.CompilerParams(
            collective_id=0, has_side_effects=True, vmem_limit_bytes=48 << 20
        ),
    )(projections, tile_mask)


def solution(mesh):
    return jax.shard_map(
        body,
        mesh=mesh,
        in_specs=(P(("clip", "seq", "tp"), None, None), P("clip", None, None)),
        out_specs=P(("clip", "seq", "tp"), None),
        check_vma=False,
    )
```

```python
import functools
import math

import jax
import jax.numpy as jnp
from jax import lax
from jax.experimental import pallas as pl
from jax.experimental.pallas import tpu as pltpu
from jax.sharding import PartitionSpec as P

MESH = pl.DeviceIdType.MESH
NEGATIVE_FILL = -1e30
CHIPS = 8
CORES = 2
PEERS = CHIPS * CORES
REACH = (1, 7, 2, 6, 3, 5, 4)
OFFSETS = tuple((d, f) for d in REACH for f in range(CORES)) + ((0, 1),)


def kernel(
    x_ref,
    mask_ref,
    out_ref,
    x_in,
    mask_in,
    qkv_out,
    qkv_got,
    o_out,
    tile_of_key,
    bias,
    scores,
    in_sem,
    mask_sem,
    own_sem,
    send_sem,
    recv_sem,
):
    y = lax.axis_index("seq")
    core = lax.axis_index("tp")
    me = y * CORES + core
    tokens, _, width = x_ref.shape
    slots = x_in.shape[0]
    dim = width // 3
    pair = CORES * tokens
    keys = qkv_got.shape[1]

    x_copies = [
        pltpu.make_async_copy(
            x_ref.at[:, pl.ds(slot * PEERS, PEERS), :], x_in.at[slot], in_sem.at[slot]
        )
        for slot in range(slots)
    ]
    x_copies[0].start()

    def peer(d, f):
        return {"seq": lax.rem(y + d, CHIPS), "tp": lax.rem(core + f, CORES)}

    def index_of(d, f):
        return lax.rem(y + d, CHIPS) * CORES + lax.rem(core + f, CORES)

    barrier = pltpu.get_barrier_semaphore()
    for d, f in OFFSETS:
        pl.semaphore_signal(barrier, inc=1, device_id=peer(d, f), device_id_type=MESH)
    for copy in x_copies[1:]:
        copy.start()
    mask_copy = pltpu.make_async_copy(mask_ref, mask_in, mask_sem)
    mask_copy.start()

    def rows_of(device):
        return pl.ds(pl.multiple_of(device * tokens, tokens), tokens)

    def ends(kind, slot, to):
        if kind == "qkv":
            return qkv_out.at[slot, to], qkv_got.at[slot, rows_of(me)], slot
        columns = pl.ds(pl.multiple_of((slot * PEERS + me) * dim, dim), dim)
        return o_out.at[slot, rows_of(to)], out_ref.at[:, columns], slots + slot

    def remote(kind, slot, d, f):
        src, dst, row = ends(kind, slot, index_of(d, f))
        number = d * CORES + f
        return pltpu.make_async_remote_copy(
            src_ref=src,
            dst_ref=dst,
            send_sem=send_sem.at[row, number],
            recv_sem=recv_sem.at[row, number],
            device_id=peer(d, f),
            device_id_type=MESH,
        )

    def own(kind, slot):
        src, dst, row = ends(kind, slot, me)
        return pltpu.make_async_copy(src, dst, own_sem.at[row])

    side = PEERS * PEERS
    to_row = lax.broadcasted_iota(jnp.int32, (side, side), 0)
    from_row = lax.broadcasted_iota(jnp.int32, (side, side), 1)
    swap = (from_row == (to_row % PEERS) * PEERS + to_row // PEERS).astype(jnp.bfloat16)

    def regroup(slot):
        for start in range(0, tokens, PEERS):
            block = x_in[slot, start : start + PEERS].reshape(side, width)
            swapped = jnp.dot(swap, block, preferred_element_type=jnp.float32)
            qkv_out[slot, :, start : start + PEERS, :] = swapped.astype(jnp.bfloat16).reshape(
                PEERS, PEERS, width
            )

    for slot in range(slots):
        x_copies[slot].wait()
        regroup(slot)
        if slot == 0:
            pl.semaphore_wait(barrier, len(OFFSETS))
        for d, f in OFFSETS:
            remote("qkv", slot, d, f).start()
        own("qkv", slot).start()

    tile_of_key[...] = (
        lax.broadcasted_iota(jnp.int32, tile_of_key.shape, 0) // tokens
        == lax.broadcasted_iota(jnp.int32, tile_of_key.shape, 1)
    ).astype(jnp.bfloat16)
    bias[...] = jnp.zeros_like(bias)
    mask_copy.wait()
    heads = mask_in.shape[2]
    my_head = lax.broadcasted_iota(jnp.int32, (8, heads), 0) * PEERS + me
    pick = (my_head == lax.broadcasted_iota(jnp.int32, (8, heads), 1)).astype(jnp.bfloat16)
    for tile in range(PEERS):
        allowed = lax.dot_general(
            pick,
            (mask_in[tile] > 0).astype(jnp.bfloat16),
            (((1,), (1,)), ((), ())),
            preferred_element_type=jnp.float32,
        )
        bias[tile, :, 0:PEERS] = jnp.where(allowed > 0.5, 0.0, NEGATIVE_FILL)

    exponent_scale = math.log2(math.e) / math.sqrt(dim)
    ones = jnp.ones((2 * dim, dim), jnp.bfloat16)
    step = 2 * dim

    def attend(slot, chip):
        rows = pl.ds(pl.multiple_of(chip * pair, pair), pair)
        biases = jnp.concatenate(
            [
                jnp.broadcast_to(bias[chip * CORES + i, slot : slot + 1, :], (tokens, dim))
                for i in range(CORES)
            ],
            axis=0,
        )
        queries = jnp.concatenate([qkv_got[slot, rows, 0:dim], biases.astype(jnp.bfloat16)], axis=1)
        largest = None
        for start in range(0, keys, step):
            part = slice(start, start + step)
            key_part = jnp.concatenate([qkv_got[slot, part, dim : 2 * dim], tile_of_key[part, :]], axis=1)
            found = lax.dot_general(
                queries, key_part, (((1,), (1,)), ((), ())), preferred_element_type=jnp.float32
            )
            scores[:, part] = found
            higher = jnp.maximum(found[:, 0:dim], found[:, dim:step])
            largest = higher if largest is None else jnp.maximum(largest, higher)
        row_max = jnp.max(largest, axis=1, keepdims=True)
        total = jnp.zeros((pair, 2 * dim), jnp.float32)
        for start in range(0, keys, step):
            part = slice(start, start + step)
            weights = jnp.exp2((scores[:, part] - row_max) * exponent_scale).astype(jnp.bfloat16)
            values = jnp.concatenate([qkv_got[slot, part, 2 * dim : 3 * dim], ones], axis=1)
            total += jnp.dot(weights, values, preferred_element_type=jnp.float32)
        o_out[slot, rows, :] = (total[:, 0:dim] / total[:, dim : 2 * dim]).astype(jnp.bfloat16)

    for slot in range(slots):
        own("qkv", slot).wait()
        for d, f in OFFSETS:
            remote("qkv", slot, d, f).wait_recv()
        attend(slot, y)
        own("o", slot).start()
        remote("o", slot, 0, 1).start()

        def turn(number, carry, slot=slot):
            distance = (number + 2) // 2
            d = jnp.where(number % 2 == 0, distance, CHIPS - distance)
            attend(slot, lax.rem(y + d, CHIPS))
            for f in range(CORES):
                remote("o", slot, d, f).start()
            return carry

        lax.fori_loop(0, CHIPS - 1, turn, 0)

    for kind in ("qkv", "o"):
        for slot in range(slots):
            if kind == "o":
                own("o", slot).wait()
            for d, f in OFFSETS:
                remote(kind, slot, d, f).wait_send()
    for slot in range(slots):
        for d, f in OFFSETS:
            remote("o", slot, d, f).wait_recv()


def body(projections, tile_mask):
    tokens, heads, width = projections.shape
    dim = width // 3
    slots = heads // PEERS
    keys = tokens * PEERS
    return pl.pallas_call(
        kernel,
        out_shape=jax.ShapeDtypeStruct((tokens, heads * dim), jnp.bfloat16),
        in_specs=[pl.BlockSpec(memory_space=pltpu.HBM)] * 2,
        out_specs=pl.BlockSpec(memory_space=pl.ANY),
        scratch_shapes=[
            pltpu.VMEM((slots, tokens, PEERS, width), jnp.bfloat16),
            pltpu.VMEM((PEERS, PEERS, heads), jnp.int32),
            pltpu.VMEM((slots, PEERS, tokens, width), jnp.bfloat16),
            pltpu.VMEM((slots, keys, width), jnp.bfloat16),
            pltpu.VMEM((slots, keys, dim), jnp.bfloat16),
            pltpu.VMEM((keys, dim), jnp.bfloat16),
            pltpu.VMEM((PEERS, 8, dim), jnp.float32),
            pltpu.VMEM((CORES * tokens, keys), jnp.float32),
            pltpu.SemaphoreType.DMA((slots,)),
            pltpu.SemaphoreType.DMA,
            pltpu.SemaphoreType.DMA((2 * slots,)),
            pltpu.SemaphoreType.DMA((2 * slots, PEERS)),
            pltpu.SemaphoreType.DMA((2 * slots, PEERS)),
        ],
        compiler_params=pltpu.CompilerParams(
            collective_id=0, has_side_effects=True, vmem_limit_bytes=48 << 20
        ),
    )(
        pltpu.with_memory_space_constraint(projections, pltpu.HBM),
        pltpu.with_memory_space_constraint(jnp.transpose(tile_mask, (1, 2, 0)), pltpu.HBM),
    )


def solution(mesh):
    return jax.shard_map(
        body,
        mesh=mesh,
        in_specs=(P(("clip", "seq", "tp"), None, None), P("clip", None, None)),
        out_specs=P(("clip", "seq", "tp"), None),
        check_vma=False,
    )
```

```python
import functools
import math

import jax
import jax.numpy as jnp
from jax import lax
from jax.experimental import pallas as pl
from jax.experimental.pallas import tpu as pltpu
from jax.sharding import PartitionSpec as P

MESH = pl.DeviceIdType.MESH
NEGATIVE_FILL = -1e30
CHIPS = 8
CORES = 2
PEERS = CHIPS * CORES
LAST = 0
REACH = (1, 7, 2, 6, 3, 5, 4)
OFFSETS = tuple((d, f) for d in REACH for f in range(CORES)) + ((0, 1),)


def kernel(
    x_ref,
    mask_ref,
    out_ref,
    x_in,
    mask_in,
    qkv_out,
    qkv_got,
    o_out,
    tile_of_key,
    bias,
    scores,
    in_sem,
    mask_sem,
    own_sem,
    send_sem,
    recv_sem,
    ready_sem,
):
    y = lax.axis_index("seq")
    core = lax.axis_index("tp")
    me = y * CORES + core
    tokens, _, width = x_ref.shape
    slots = x_in.shape[0]
    dim = width // 3
    pair = CORES * tokens
    keys = qkv_got.shape[1]

    x_copies = [
        pltpu.make_async_copy(
            x_ref.at[:, pl.ds(slot * PEERS, PEERS), :], x_in.at[slot], in_sem.at[slot]
        )
        for slot in range(slots)
    ]
    x_copies[0].start()

    def peer(d, f):
        return {"seq": lax.rem(y + d, CHIPS), "tp": lax.rem(core + f, CORES)}

    def index_of(d, f):
        return lax.rem(y + d, CHIPS) * CORES + lax.rem(core + f, CORES)

    barrier = pltpu.get_barrier_semaphore()

    @pl.when(me != LAST)
    def _():
        for d, f in OFFSETS:
            pl.semaphore_signal(barrier, inc=1, device_id=peer(d, f), device_id_type=MESH)

    for copy in x_copies[1:]:
        copy.start()
    mask_copy = pltpu.make_async_copy(mask_ref, mask_in, mask_sem)
    mask_copy.start()

    def rows_of(device):
        return pl.ds(pl.multiple_of(device * tokens, tokens), tokens)

    def ends(kind, slot, to):
        if kind == "qkv":
            return qkv_out.at[slot, to], qkv_got.at[slot, rows_of(me)], slot
        columns = pl.ds(pl.multiple_of((slot * PEERS + me) * dim, dim), dim)
        return o_out.at[slot, rows_of(to)], out_ref.at[:, columns], slots + slot

    def remote(kind, slot, d, f):
        src, dst, row = ends(kind, slot, index_of(d, f))
        number = d * CORES + f
        return pltpu.make_async_remote_copy(
            src_ref=src,
            dst_ref=dst,
            send_sem=send_sem.at[row, number],
            recv_sem=recv_sem.at[row, number],
            device_id=peer(d, f),
            device_id_type=MESH,
        )

    def own(kind, slot):
        src, dst, row = ends(kind, slot, me)
        return pltpu.make_async_copy(src, dst, own_sem.at[row])

    side = PEERS * PEERS
    to_row = lax.broadcasted_iota(jnp.int32, (side, side), 0)
    from_row = lax.broadcasted_iota(jnp.int32, (side, side), 1)
    swap = (from_row == (to_row % PEERS) * PEERS + to_row // PEERS).astype(jnp.bfloat16)

    def regroup(slot):
        for start in range(0, tokens, PEERS):
            block = x_in[slot, start : start + PEERS].reshape(side, width)
            swapped = jnp.dot(swap, block, preferred_element_type=jnp.float32)
            qkv_out[slot, :, start : start + PEERS, :] = swapped.astype(jnp.bfloat16).reshape(
                PEERS, PEERS, width
            )

    x_copies[0].wait()
    regroup(0)

    @pl.when(me != LAST)
    def _():
        pl.semaphore_wait(barrier, len(OFFSETS) - 1)

    @pl.when(me == LAST)
    def _():
        pl.semaphore_wait(barrier, len(OFFSETS))
        for d, f in OFFSETS:
            pl.semaphore_signal(ready_sem, inc=1, device_id=peer(d, f), device_id_type=MESH)

    for d, f in OFFSETS:

        @pl.when(index_of(d, f) != LAST)
        def _(d=d, f=f):
            remote("qkv", 0, d, f).start()

    own("qkv", 0).start()
    x_copies[1].wait()
    regroup(1)

    @pl.when(me != LAST)
    def _():
        pl.semaphore_wait(ready_sem, 1)
        d = lax.rem(LAST // CORES + CHIPS - y, CHIPS)
        f = lax.rem(LAST % CORES + CORES - core, CORES)
        remote("qkv", 0, d, f).start()

    for d, f in OFFSETS:
        remote("qkv", 1, d, f).start()
    own("qkv", 1).start()

    tile_of_key[...] = (
        lax.broadcasted_iota(jnp.int32, tile_of_key.shape, 0) // tokens
        == lax.broadcasted_iota(jnp.int32, tile_of_key.shape, 1)
    ).astype(jnp.bfloat16)
    bias[...] = jnp.zeros_like(bias)
    mask_copy.wait()
    heads = mask_in.shape[2]
    my_head = lax.broadcasted_iota(jnp.int32, (8, heads), 0) * PEERS + me
    pick = (my_head == lax.broadcasted_iota(jnp.int32, (8, heads), 1)).astype(jnp.bfloat16)
    for tile in range(PEERS):
        allowed = lax.dot_general(
            pick,
            (mask_in[tile] > 0).astype(jnp.bfloat16),
            (((1,), (1,)), ((), ())),
            preferred_element_type=jnp.float32,
        )
        bias[tile, :, 0:PEERS] = jnp.where(allowed > 0.5, 0.0, NEGATIVE_FILL)

    exponent_scale = math.log2(math.e) / math.sqrt(dim)
    ones = jnp.ones((2 * dim, dim), jnp.bfloat16)
    step = 2 * dim

    def attend(slot, chip):
        rows = pl.ds(pl.multiple_of(chip * pair, pair), pair)
        biases = jnp.concatenate(
            [
                jnp.broadcast_to(bias[chip * CORES + i, slot : slot + 1, :], (tokens, dim))
                for i in range(CORES)
            ],
            axis=0,
        )
        queries = jnp.concatenate([qkv_got[slot, rows, 0:dim], biases.astype(jnp.bfloat16)], axis=1)
        largest = None
        for start in range(0, keys, step):
            part = slice(start, start + step)
            key_part = jnp.concatenate([qkv_got[slot, part, dim : 2 * dim], tile_of_key[part, :]], axis=1)
            found = lax.dot_general(
                queries, key_part, (((1,), (1,)), ((), ())), preferred_element_type=jnp.float32
            )
            scores[:, part] = found
            higher = jnp.maximum(found[:, 0:dim], found[:, dim:step])
            largest = higher if largest is None else jnp.maximum(largest, higher)
        row_max = jnp.max(largest, axis=1, keepdims=True)
        total = jnp.zeros((pair, 2 * dim), jnp.float32)
        for start in range(0, keys, step):
            part = slice(start, start + step)
            weights = jnp.exp2((scores[:, part] - row_max) * exponent_scale).astype(jnp.bfloat16)
            values = jnp.concatenate([qkv_got[slot, part, 2 * dim : 3 * dim], ones], axis=1)
            total += jnp.dot(weights, values, preferred_element_type=jnp.float32)
        o_out[slot, rows, :] = (total[:, 0:dim] / total[:, dim : 2 * dim]).astype(jnp.bfloat16)

    for slot in range(slots):
        own("qkv", slot).wait()
        for d, f in OFFSETS:
            remote("qkv", slot, d, f).wait_recv()
        attend(slot, y)
        own("o", slot).start()
        remote("o", slot, 0, 1).start()

        def turn(number, carry, slot=slot):
            distance = (number + 2) // 2
            d = jnp.where(number % 2 == 0, distance, CHIPS - distance)
            attend(slot, lax.rem(y + d, CHIPS))
            for f in range(CORES):
                remote("o", slot, d, f).start()
            return carry

        lax.fori_loop(0, CHIPS - 1, turn, 0)

    for kind in ("qkv", "o"):
        for slot in range(slots):
            if kind == "o":
                own("o", slot).wait()
            for d, f in OFFSETS:
                remote(kind, slot, d, f).wait_send()
    for slot in range(slots):
        for d, f in OFFSETS:
            remote("o", slot, d, f).wait_recv()


def body(projections, tile_mask):
    tokens, heads, width = projections.shape
    dim = width // 3
    slots = heads // PEERS
    keys = tokens * PEERS
    return pl.pallas_call(
        kernel,
        out_shape=jax.ShapeDtypeStruct((tokens, heads * dim), jnp.bfloat16),
        in_specs=[pl.BlockSpec(memory_space=pltpu.HBM)] * 2,
        out_specs=pl.BlockSpec(memory_space=pl.ANY),
        scratch_shapes=[
            pltpu.VMEM((slots, tokens, PEERS, width), jnp.bfloat16),
            pltpu.VMEM((PEERS, PEERS, heads), jnp.int32),
            pltpu.VMEM((slots, PEERS, tokens, width), jnp.bfloat16),
            pltpu.VMEM((slots, keys, width), jnp.bfloat16),
            pltpu.VMEM((slots, keys, dim), jnp.bfloat16),
            pltpu.VMEM((keys, dim), jnp.bfloat16),
            pltpu.VMEM((PEERS, 8, dim), jnp.float32),
            pltpu.VMEM((CORES * tokens, keys), jnp.float32),
            pltpu.SemaphoreType.DMA((slots,)),
            pltpu.SemaphoreType.DMA,
            pltpu.SemaphoreType.DMA((2 * slots,)),
            pltpu.SemaphoreType.DMA((2 * slots, PEERS)),
            pltpu.SemaphoreType.DMA((2 * slots, PEERS)),
            pltpu.SemaphoreType.REGULAR,
        ],
        compiler_params=pltpu.CompilerParams(
            collective_id=0, has_side_effects=True, vmem_limit_bytes=48 << 20
        ),
    )(
        pltpu.with_memory_space_constraint(projections, pltpu.HBM),
        pltpu.with_memory_space_constraint(jnp.transpose(tile_mask, (1, 2, 0)), pltpu.HBM),
    )


def solution(mesh):
    return jax.shard_map(
        body,
        mesh=mesh,
        in_specs=(P(("clip", "seq", "tp"), None, None), P("clip", None, None)),
        out_specs=P(("clip", "seq", "tp"), None),
        check_vma=False,
    )
```

```python
import functools
import math

import jax
import jax.numpy as jnp
from jax import lax
from jax.experimental import pallas as pl
from jax.experimental.pallas import tpu as pltpu
from jax.sharding import PartitionSpec as P

MESH = pl.DeviceIdType.MESH
NEGATIVE_FILL = -1e30
CHIPS = 8
CORES = 2
PEERS = CHIPS * CORES
LAST = 0
REACH = (1, 7, 2, 6, 3, 5, 4)
OFFSETS = tuple((d, f) for d in REACH for f in range(CORES)) + ((0, 1),)


def kernel(
    x_ref,
    mask_ref,
    out_ref,
    x_in,
    mask_in,
    qkv_out,
    qkv_got,
    o_out,
    tile_of_key,
    bias,
    scores,
    in_sem,
    mask_sem,
    own_sem,
    send_sem,
    recv_sem,
    ready_sem,
):
    y = lax.axis_index("seq")
    core = lax.axis_index("tp")
    me = y * CORES + core
    tokens, _, width = x_ref.shape
    slots = x_in.shape[0]
    dim = width // 3
    pair = CORES * tokens
    keys = qkv_got.shape[1]

    x_copies = [
        pltpu.make_async_copy(
            x_ref.at[:, pl.ds(slot * PEERS, PEERS), :], x_in.at[slot], in_sem.at[slot]
        )
        for slot in range(slots)
    ]
    x_copies[0].start()

    def peer(d, f):
        return {"seq": lax.rem(y + d, CHIPS), "tp": lax.rem(core + f, CORES)}

    def index_of(d, f):
        return lax.rem(y + d, CHIPS) * CORES + lax.rem(core + f, CORES)

    barrier = pltpu.get_barrier_semaphore()

    @pl.when(me != LAST)
    def _():
        for d, f in OFFSETS:
            pl.semaphore_signal(barrier, inc=1, device_id=peer(d, f), device_id_type=MESH)

    for copy in x_copies[1:]:
        copy.start()
    mask_copy = pltpu.make_async_copy(mask_ref, mask_in, mask_sem)
    mask_copy.start()

    def rows_of(device):
        return pl.ds(pl.multiple_of(device * tokens, tokens), tokens)

    def ends(kind, slot, to):
        if kind == "qkv":
            return qkv_out.at[slot, to], qkv_got.at[slot, rows_of(me)], slot
        columns = pl.ds(pl.multiple_of((slot * PEERS + me) * dim, dim), dim)
        return o_out.at[slot, rows_of(to)], out_ref.at[:, columns], slots

    def remote(kind, slot, d, f):
        src, dst, number = ends(kind, slot, index_of(d, f))
        return pltpu.make_async_remote_copy(
            src_ref=src,
            dst_ref=dst,
            send_sem=send_sem.at[number],
            recv_sem=recv_sem.at[number],
            device_id=peer(d, f),
            device_id_type=MESH,
        )

    def all_of(kind, slot=0):
        others = PEERS - 1
        if kind == "qkv":
            src, dst, number = qkv_out.at[slot, 0:others], qkv_got.at[slot, 0 : others * tokens], slot
        else:
            src = o_out.at[:, 0 : others * tokens]
            dst, number = out_ref.at[:, 0 : slots * others * dim], slots
        return pltpu.make_async_remote_copy(
            src_ref=src,
            dst_ref=dst,
            send_sem=send_sem.at[number],
            recv_sem=recv_sem.at[number],
            device_id=peer(0, 1),
            device_id_type=MESH,
        )

    def own(kind, slot):
        src, dst, number = ends(kind, slot, me)
        return pltpu.make_async_copy(src, dst, own_sem.at[number + slot if kind == "o" else number])

    side = PEERS * PEERS
    to_row = lax.broadcasted_iota(jnp.int32, (side, side), 0)
    from_row = lax.broadcasted_iota(jnp.int32, (side, side), 1)
    swap = (from_row == (to_row % PEERS) * PEERS + to_row // PEERS).astype(jnp.bfloat16)

    def regroup(slot):
        for start in range(0, tokens, PEERS):
            block = x_in[slot, start : start + PEERS].reshape(side, width)
            swapped = jnp.dot(swap, block, preferred_element_type=jnp.float32)
            qkv_out[slot, :, start : start + PEERS, :] = swapped.astype(jnp.bfloat16).reshape(
                PEERS, PEERS, width
            )

    x_copies[0].wait()
    regroup(0)

    @pl.when(me != LAST)
    def _():
        pl.semaphore_wait(barrier, len(OFFSETS) - 1)

    @pl.when(me == LAST)
    def _():
        pl.semaphore_wait(barrier, len(OFFSETS))
        for d, f in OFFSETS:
            pl.semaphore_signal(ready_sem, inc=1, device_id=peer(d, f), device_id_type=MESH)

    for d, f in OFFSETS:

        @pl.when(index_of(d, f) != LAST)
        def _(d=d, f=f):
            remote("qkv", 0, d, f).start()

    own("qkv", 0).start()
    x_copies[1].wait()
    regroup(1)

    @pl.when(me != LAST)
    def _():
        pl.semaphore_wait(ready_sem, 1)
        d = lax.rem(LAST // CORES + CHIPS - y, CHIPS)
        f = lax.rem(LAST % CORES + CORES - core, CORES)
        remote("qkv", 0, d, f).start()

    for d, f in OFFSETS:
        remote("qkv", 1, d, f).start()
    own("qkv", 1).start()

    tile_of_key[...] = (
        lax.broadcasted_iota(jnp.int32, tile_of_key.shape, 0) // tokens
        == lax.broadcasted_iota(jnp.int32, tile_of_key.shape, 1)
    ).astype(jnp.bfloat16)
    bias[...] = jnp.zeros_like(bias)
    mask_copy.wait()
    heads = mask_in.shape[2]
    my_head = lax.broadcasted_iota(jnp.int32, (8, heads), 0) * PEERS + me
    pick = (my_head == lax.broadcasted_iota(jnp.int32, (8, heads), 1)).astype(jnp.bfloat16)
    for tile in range(PEERS):
        allowed = lax.dot_general(
            pick,
            (mask_in[tile] > 0).astype(jnp.bfloat16),
            (((1,), (1,)), ((), ())),
            preferred_element_type=jnp.float32,
        )
        bias[tile, :, 0:PEERS] = jnp.where(allowed > 0.5, 0.0, NEGATIVE_FILL)

    exponent_scale = math.log2(math.e) / math.sqrt(dim)
    ones = jnp.ones((2 * dim, dim), jnp.bfloat16)
    step = 2 * dim

    def attend(slot, chip):
        rows = pl.ds(pl.multiple_of(chip * pair, pair), pair)
        biases = jnp.concatenate(
            [
                jnp.broadcast_to(bias[chip * CORES + i, slot : slot + 1, :], (tokens, dim))
                for i in range(CORES)
            ],
            axis=0,
        )
        queries = jnp.concatenate([qkv_got[slot, rows, 0:dim], biases.astype(jnp.bfloat16)], axis=1)
        largest = None
        for start in range(0, keys, step):
            part = slice(start, start + step)
            key_part = jnp.concatenate([qkv_got[slot, part, dim : 2 * dim], tile_of_key[part, :]], axis=1)
            found = lax.dot_general(
                queries, key_part, (((1,), (1,)), ((), ())), preferred_element_type=jnp.float32
            )
            scores[:, part] = found
            higher = jnp.maximum(found[:, 0:dim], found[:, dim:step])
            largest = higher if largest is None else jnp.maximum(largest, higher)
        row_max = jnp.max(largest, axis=1, keepdims=True)
        total = jnp.zeros((pair, 2 * dim), jnp.float32)
        for start in range(0, keys, step):
            part = slice(start, start + step)
            weights = jnp.exp2((scores[:, part] - row_max) * exponent_scale).astype(jnp.bfloat16)
            values = jnp.concatenate([qkv_got[slot, part, 2 * dim : 3 * dim], ones], axis=1)
            total += jnp.dot(weights, values, preferred_element_type=jnp.float32)
        o_out[slot, rows, :] = (total[:, 0:dim] / total[:, dim : 2 * dim]).astype(jnp.bfloat16)

    for slot in range(slots):
        own("qkv", slot).wait()
        all_of("qkv", slot).wait_recv()
        attend(slot, y)
        own("o", slot).start()
        remote("o", slot, 0, 1).start()

        def turn(number, carry, slot=slot):
            distance = (number + 2) // 2
            d = jnp.where(number % 2 == 0, distance, CHIPS - distance)
            attend(slot, lax.rem(y + d, CHIPS))
            for f in range(CORES):
                remote("o", slot, d, f).start()
            return carry

        lax.fori_loop(0, CHIPS - 1, turn, 0)

    for slot in range(slots):
        all_of("qkv", slot).wait_send()
        own("o", slot).wait()
    all_of("o").wait_send()
    all_of("o").wait_recv()


def body(projections, tile_mask):
    tokens, heads, width = projections.shape
    dim = width // 3
    slots = heads // PEERS
    keys = tokens * PEERS
    return pl.pallas_call(
        kernel,
        out_shape=jax.ShapeDtypeStruct((tokens, heads * dim), jnp.bfloat16),
        in_specs=[pl.BlockSpec(memory_space=pltpu.HBM)] * 2,
        out_specs=pl.BlockSpec(memory_space=pl.ANY),
        scratch_shapes=[
            pltpu.VMEM((slots, tokens, PEERS, width), jnp.bfloat16),
            pltpu.VMEM((PEERS, PEERS, heads), jnp.int32),
            pltpu.VMEM((slots, PEERS, tokens, width), jnp.bfloat16),
            pltpu.VMEM((slots, keys, width), jnp.bfloat16),
            pltpu.VMEM((slots, keys, dim), jnp.bfloat16),
            pltpu.VMEM((keys, dim), jnp.bfloat16),
            pltpu.VMEM((PEERS, 8, dim), jnp.float32),
            pltpu.VMEM((CORES * tokens, keys), jnp.float32),
            pltpu.SemaphoreType.DMA((slots,)),
            pltpu.SemaphoreType.DMA,
            pltpu.SemaphoreType.DMA((2 * slots,)),
            pltpu.SemaphoreType.DMA((slots + 1,)),
            pltpu.SemaphoreType.DMA((slots + 1,)),
            pltpu.SemaphoreType.REGULAR,
        ],
        compiler_params=pltpu.CompilerParams(
            collective_id=0, has_side_effects=True, vmem_limit_bytes=48 << 20
        ),
    )(
        pltpu.with_memory_space_constraint(projections, pltpu.HBM),
        pltpu.with_memory_space_constraint(jnp.transpose(tile_mask, (1, 2, 0)), pltpu.HBM),
    )


def solution(mesh):
    return jax.shard_map(
        body,
        mesh=mesh,
        in_specs=(P(("clip", "seq", "tp"), None, None), P("clip", None, None)),
        out_specs=P(("clip", "seq", "tp"), None),
        check_vma=False,
    )
```

```python
import functools
import math

import jax
import jax.numpy as jnp
from jax import lax
from jax.experimental import pallas as pl
from jax.experimental.pallas import tpu as pltpu
from jax.sharding import PartitionSpec as P

MESH = pl.DeviceIdType.MESH
NEGATIVE_FILL = -1e30
CHIPS = 8
CORES = 2
PEERS = CHIPS * CORES
LATE = (0, 8, 9, 10, 11)
TELLS = ((1, 0), (6, 8), (7, 9), (12, 10), (13, 11))
REACH = (1, 7, 2, 6, 3, 5, 4)
OFFSETS = tuple((d, f) for d in REACH for f in range(CORES)) + ((0, 1),)


def kernel(
    x_ref,
    mask_ref,
    out_ref,
    x_in,
    mask_in,
    qkv_out,
    qkv_got,
    o_out,
    tile_of_key,
    bias,
    scores,
    in_sem,
    mask_sem,
    own_sem,
    send_sem,
    recv_sem,
    ready_sem,
):
    y = lax.axis_index("seq")
    core = lax.axis_index("tp")
    me = y * CORES + core
    tokens, _, width = x_ref.shape
    slots = x_in.shape[0]
    dim = width // 3
    pair = CORES * tokens
    keys = qkv_got.shape[1]

    x_copies = [
        pltpu.make_async_copy(
            x_ref.at[:, pl.ds(slot * PEERS, PEERS), :], x_in.at[slot], in_sem.at[slot]
        )
        for slot in range(slots)
    ]
    x_copies[0].start()

    def peer(d, f):
        return {"seq": lax.rem(y + d, CHIPS), "tp": lax.rem(core + f, CORES)}

    def index_of(d, f):
        return lax.rem(y + d, CHIPS) * CORES + lax.rem(core + f, CORES)

    def is_late(device):
        return functools.reduce(jnp.logical_or, [device == late for late in LATE])

    barrier = pltpu.get_barrier_semaphore()
    late = is_late(me)
    early = jnp.logical_not(late)

    @pl.when(early)
    def _():
        for d, f in OFFSETS:
            pl.semaphore_signal(barrier, inc=1, device_id=peer(d, f), device_id_type=MESH)

    for copy in x_copies[1:]:
        copy.start()
    mask_copy = pltpu.make_async_copy(mask_ref, mask_in, mask_sem)
    mask_copy.start()

    def rows_of(device):
        return pl.ds(pl.multiple_of(device * tokens, tokens), tokens)

    def ends(kind, slot, to):
        if kind == "qkv":
            return qkv_out.at[slot, to], qkv_got.at[slot, rows_of(me)], slot
        columns = pl.ds(pl.multiple_of((slot * PEERS + me) * dim, dim), dim)
        return o_out.at[slot, rows_of(to)], out_ref.at[:, columns], slots

    def remote(kind, slot, d, f):
        src, dst, number = ends(kind, slot, index_of(d, f))
        return pltpu.make_async_remote_copy(
            src_ref=src,
            dst_ref=dst,
            send_sem=send_sem.at[number],
            recv_sem=recv_sem.at[number],
            device_id=peer(d, f),
            device_id_type=MESH,
        )

    def all_of(kind, slot=0):
        others = PEERS - 1
        if kind == "qkv":
            src, dst, number = qkv_out.at[slot, 0:others], qkv_got.at[slot, 0 : others * tokens], slot
        else:
            src = o_out.at[:, 0 : others * tokens]
            dst, number = out_ref.at[:, 0 : slots * others * dim], slots
        return pltpu.make_async_remote_copy(
            src_ref=src,
            dst_ref=dst,
            send_sem=send_sem.at[number],
            recv_sem=recv_sem.at[number],
            device_id=peer(0, 1),
            device_id_type=MESH,
        )

    def own(kind, slot):
        src, dst, number = ends(kind, slot, me)
        return pltpu.make_async_copy(src, dst, own_sem.at[number + slot if kind == "o" else number])

    side = PEERS * PEERS
    to_row = lax.broadcasted_iota(jnp.int32, (side, side), 0)
    from_row = lax.broadcasted_iota(jnp.int32, (side, side), 1)
    swap = (from_row == (to_row % PEERS) * PEERS + to_row // PEERS).astype(jnp.bfloat16)

    def regroup(slot):
        for start in range(0, tokens, PEERS):
            block = x_in[slot, start : start + PEERS].reshape(side, width)
            swapped = jnp.dot(swap, block, preferred_element_type=jnp.float32)
            qkv_out[slot, :, start : start + PEERS, :] = swapped.astype(jnp.bfloat16).reshape(
                PEERS, PEERS, width
            )

    x_copies[0].wait()
    regroup(0)

    @pl.when(early)
    def _():
        pl.semaphore_wait(barrier, PEERS - len(LATE) - 1)

    @pl.when(late)
    def _():
        pl.semaphore_wait(barrier, PEERS - len(LATE))
        for d, f in OFFSETS:

            @pl.when(jnp.logical_not(is_late(index_of(d, f))))
            def _(d=d, f=f):
                pl.semaphore_signal(ready_sem, inc=1, device_id=peer(d, f), device_id_type=MESH)

    for d, f in OFFSETS:

        @pl.when(jnp.logical_not(is_late(index_of(d, f))))
        def _(d=d, f=f):
            remote("qkv", 0, d, f).start()

    own("qkv", 0).start()
    x_copies[1].wait()
    regroup(1)

    @pl.when(early)
    def _():
        pl.semaphore_wait(ready_sem, len(LATE))
        for teller, told in TELLS:

            @pl.when(me == teller)
            def _(told=told):
                pl.semaphore_signal(
                    ready_sem,
                    inc=1,
                    device_id={"seq": told // CORES, "tp": told % CORES},
                    device_id_type=MESH,
                )

    @pl.when(late)
    def _():
        pl.semaphore_wait(ready_sem, 1)

    for d, f in OFFSETS:

        @pl.when(is_late(index_of(d, f)))
        def _(d=d, f=f):
            remote("qkv", 0, d, f).start()

    for d, f in OFFSETS:
        remote("qkv", 1, d, f).start()
    own("qkv", 1).start()

    tile_of_key[...] = (
        lax.broadcasted_iota(jnp.int32, tile_of_key.shape, 0) // tokens
        == lax.broadcasted_iota(jnp.int32, tile_of_key.shape, 1)
    ).astype(jnp.bfloat16)
    bias[...] = jnp.zeros_like(bias)
    mask_copy.wait()
    heads = mask_in.shape[2]
    my_head = lax.broadcasted_iota(jnp.int32, (8, heads), 0) * PEERS + me
    pick = (my_head == lax.broadcasted_iota(jnp.int32, (8, heads), 1)).astype(jnp.bfloat16)
    for tile in range(PEERS):
        allowed = lax.dot_general(
            pick,
            (mask_in[tile] > 0).astype(jnp.bfloat16),
            (((1,), (1,)), ((), ())),
            preferred_element_type=jnp.float32,
        )
        bias[tile, :, 0:PEERS] = jnp.where(allowed > 0.5, 0.0, NEGATIVE_FILL)

    exponent_scale = math.log2(math.e) / math.sqrt(dim)
    ones = jnp.ones((2 * dim, dim), jnp.bfloat16)
    step = 2 * dim

    def attend(slot, chip):
        rows = pl.ds(pl.multiple_of(chip * pair, pair), pair)
        biases = jnp.concatenate(
            [
                jnp.broadcast_to(bias[chip * CORES + i, slot : slot + 1, :], (tokens, dim))
                for i in range(CORES)
            ],
            axis=0,
        )
        queries = jnp.concatenate([qkv_got[slot, rows, 0:dim], biases.astype(jnp.bfloat16)], axis=1)
        largest = None
        for start in range(0, keys, step):
            part = slice(start, start + step)
            key_part = jnp.concatenate([qkv_got[slot, part, dim : 2 * dim], tile_of_key[part, :]], axis=1)
            found = lax.dot_general(
                queries, key_part, (((1,), (1,)), ((), ())), preferred_element_type=jnp.float32
            )
            scores[:, part] = found
            higher = jnp.maximum(found[:, 0:dim], found[:, dim:step])
            largest = higher if largest is None else jnp.maximum(largest, higher)
        row_max = jnp.max(largest, axis=1, keepdims=True)
        total = jnp.zeros((pair, 2 * dim), jnp.float32)
        for start in range(0, keys, step):
            part = slice(start, start + step)
            weights = jnp.exp2((scores[:, part] - row_max) * exponent_scale).astype(jnp.bfloat16)
            values = jnp.concatenate([qkv_got[slot, part, 2 * dim : 3 * dim], ones], axis=1)
            total += jnp.dot(weights, values, preferred_element_type=jnp.float32)
        o_out[slot, rows, :] = (total[:, 0:dim] / total[:, dim : 2 * dim]).astype(jnp.bfloat16)

    for slot in range(slots):
        own("qkv", slot).wait()
        all_of("qkv", slot).wait_recv()
        attend(slot, y)
        own("o", slot).start()
        remote("o", slot, 0, 1).start()

        def turn(number, carry, slot=slot):
            distance = (CHIPS - number) // 2
            d = jnp.where(number % 2 == 0, distance, CHIPS - distance)
            attend(slot, lax.rem(y + d, CHIPS))
            for f in range(CORES):
                remote("o", slot, d, f).start()
            return carry

        lax.fori_loop(0, CHIPS - 1, turn, 0)

    for slot in range(slots):
        all_of("qkv", slot).wait_send()
        own("o", slot).wait()
    all_of("o").wait_send()
    all_of("o").wait_recv()


def body(projections, tile_mask):
    tokens, heads, width = projections.shape
    dim = width // 3
    slots = heads // PEERS
    keys = tokens * PEERS
    return pl.pallas_call(
        kernel,
        out_shape=jax.ShapeDtypeStruct((tokens, heads * dim), jnp.bfloat16),
        in_specs=[pl.BlockSpec(memory_space=pltpu.HBM)] * 2,
        out_specs=pl.BlockSpec(memory_space=pl.ANY),
        scratch_shapes=[
            pltpu.VMEM((slots, tokens, PEERS, width), jnp.bfloat16),
            pltpu.VMEM((PEERS, PEERS, heads), jnp.int32),
            pltpu.VMEM((slots, PEERS, tokens, width), jnp.bfloat16),
            pltpu.VMEM((slots, keys, width), jnp.bfloat16),
            pltpu.VMEM((slots, keys, dim), jnp.bfloat16),
            pltpu.VMEM((keys, dim), jnp.bfloat16),
            pltpu.VMEM((PEERS, 8, dim), jnp.float32),
            pltpu.VMEM((CORES * tokens, keys), jnp.float32),
            pltpu.SemaphoreType.DMA((slots,)),
            pltpu.SemaphoreType.DMA,
            pltpu.SemaphoreType.DMA((2 * slots,)),
            pltpu.SemaphoreType.DMA((slots + 1,)),
            pltpu.SemaphoreType.DMA((slots + 1,)),
            pltpu.SemaphoreType.REGULAR,
        ],
        compiler_params=pltpu.CompilerParams(
            collective_id=0, has_side_effects=True, vmem_limit_bytes=48 << 20
        ),
    )(
        pltpu.with_memory_space_constraint(projections, pltpu.HBM),
        pltpu.with_memory_space_constraint(jnp.transpose(tile_mask, (1, 2, 0)), pltpu.HBM),
    )


def solution(mesh):
    return jax.shard_map(
        body,
        mesh=mesh,
        in_specs=(P(("clip", "seq", "tp"), None, None), P("clip", None, None)),
        out_specs=P(("clip", "seq", "tp"), None),
        check_vma=False,
    )
```

```python
import functools
import math

import jax
import jax.numpy as jnp
from jax import lax
from jax.experimental import pallas as pl
from jax.experimental.pallas import tpu as pltpu
from jax.sharding import PartitionSpec as P

MESH = pl.DeviceIdType.MESH
NEGATIVE_FILL = -1e30
CHIPS = 8
CORES = 2
PEERS = CHIPS * CORES
LATE = (0, 8, 9, 10, 11)
TELLS = ((1, 0), (6, 8), (7, 9), (12, 10), (13, 11))
REACH = (1, 7, 2, 6, 3, 5, 4)
SECOND = tuple((d, f) for d in (3, 5, 4, 2, 6, 1, 7) for f in range(CORES)) + ((0, 1),)
OFFSETS = tuple((d, f) for d in REACH for f in range(CORES)) + ((0, 1),)


def kernel(
    x_ref,
    mask_ref,
    out_ref,
    x_in,
    mask_in,
    qkv_out,
    qkv_got,
    o_out,
    tile_of_key,
    bias,
    scores,
    in_sem,
    mask_sem,
    own_sem,
    send_sem,
    recv_sem,
    ready_sem,
):
    y = lax.axis_index("seq")
    core = lax.axis_index("tp")
    me = y * CORES + core
    tokens, _, width = x_ref.shape
    slots = x_in.shape[0]
    dim = width // 3
    pair = CORES * tokens
    keys = qkv_got.shape[1]

    x_copies = [
        pltpu.make_async_copy(
            x_ref.at[:, pl.ds(slot * PEERS, PEERS), :], x_in.at[slot], in_sem.at[slot]
        )
        for slot in range(slots)
    ]
    x_copies[0].start()

    def peer(d, f):
        return {"seq": lax.rem(y + d, CHIPS), "tp": lax.rem(core + f, CORES)}

    def index_of(d, f):
        return lax.rem(y + d, CHIPS) * CORES + lax.rem(core + f, CORES)

    def is_late(device):
        return functools.reduce(jnp.logical_or, [device == late for late in LATE])

    barrier = pltpu.get_barrier_semaphore()
    late = is_late(me)
    early = jnp.logical_not(late)

    @pl.when(early)
    def _():
        for d, f in OFFSETS:
            pl.semaphore_signal(barrier, inc=1, device_id=peer(d, f), device_id_type=MESH)

    for copy in x_copies[1:]:
        copy.start()
    mask_copy = pltpu.make_async_copy(mask_ref, mask_in, mask_sem)
    mask_copy.start()

    def rows_of(device):
        return pl.ds(pl.multiple_of(device * tokens, tokens), tokens)

    def ends(kind, slot, to):
        if kind == "qkv":
            return qkv_out.at[slot, to], qkv_got.at[slot, rows_of(me)], slot
        columns = pl.ds(pl.multiple_of((slot * PEERS + me) * dim, dim), dim)
        return o_out.at[slot, rows_of(to)], out_ref.at[:, columns], slots

    def remote(kind, slot, d, f):
        src, dst, number = ends(kind, slot, index_of(d, f))
        return pltpu.make_async_remote_copy(
            src_ref=src,
            dst_ref=dst,
            send_sem=send_sem.at[number],
            recv_sem=recv_sem.at[number],
            device_id=peer(d, f),
            device_id_type=MESH,
        )

    def all_of(kind, slot=0):
        others = PEERS - 1
        if kind == "qkv":
            src, dst, number = qkv_out.at[slot, 0:others], qkv_got.at[slot, 0 : others * tokens], slot
        else:
            src = o_out.at[:, 0 : others * tokens]
            dst, number = out_ref.at[:, 0 : slots * others * dim], slots
        return pltpu.make_async_remote_copy(
            src_ref=src,
            dst_ref=dst,
            send_sem=send_sem.at[number],
            recv_sem=recv_sem.at[number],
            device_id=peer(0, 1),
            device_id_type=MESH,
        )

    def own(kind, slot):
        src, dst, number = ends(kind, slot, me)
        return pltpu.make_async_copy(src, dst, own_sem.at[number + slot if kind == "o" else number])

    side = PEERS * PEERS
    to_row = lax.broadcasted_iota(jnp.int32, (side, side), 0)
    from_row = lax.broadcasted_iota(jnp.int32, (side, side), 1)
    swap = (from_row == (to_row % PEERS) * PEERS + to_row // PEERS).astype(jnp.bfloat16)

    def regroup(slot):
        for start in range(0, tokens, PEERS):
            block = x_in[slot, start : start + PEERS].reshape(side, width)
            swapped = jnp.dot(swap, block, preferred_element_type=jnp.float32)
            qkv_out[slot, :, start : start + PEERS, :] = swapped.astype(jnp.bfloat16).reshape(
                PEERS, PEERS, width
            )

    x_copies[0].wait()
    regroup(0)

    @pl.when(early)
    def _():
        pl.semaphore_wait(barrier, PEERS - len(LATE) - 1)

    @pl.when(late)
    def _():
        pl.semaphore_wait(barrier, PEERS - len(LATE))
        for d, f in OFFSETS:

            @pl.when(jnp.logical_not(is_late(index_of(d, f))))
            def _(d=d, f=f):
                pl.semaphore_signal(ready_sem, inc=1, device_id=peer(d, f), device_id_type=MESH)

    for d, f in OFFSETS:

        @pl.when(jnp.logical_not(is_late(index_of(d, f))))
        def _(d=d, f=f):
            remote("qkv", 0, d, f).start()

    own("qkv", 0).start()
    x_copies[1].wait()
    regroup(1)

    @pl.when(early)
    def _():
        pl.semaphore_wait(ready_sem, len(LATE))
        for teller, told in TELLS:

            @pl.when(me == teller)
            def _(told=told):
                pl.semaphore_signal(
                    ready_sem,
                    inc=1,
                    device_id={"seq": told // CORES, "tp": told % CORES},
                    device_id_type=MESH,
                )

    @pl.when(late)
    def _():
        pl.semaphore_wait(ready_sem, 1)

    for d, f in OFFSETS:

        @pl.when(is_late(index_of(d, f)))
        def _(d=d, f=f):
            remote("qkv", 0, d, f).start()

    for d, f in SECOND:
        remote("qkv", 1, d, f).start()
    own("qkv", 1).start()

    tile_of_key[...] = (
        lax.broadcasted_iota(jnp.int32, tile_of_key.shape, 0) // tokens
        == lax.broadcasted_iota(jnp.int32, tile_of_key.shape, 1)
    ).astype(jnp.bfloat16)
    bias[...] = jnp.zeros_like(bias)
    mask_copy.wait()
    heads = mask_in.shape[2]
    my_head = lax.broadcasted_iota(jnp.int32, (8, heads), 0) * PEERS + me
    pick = (my_head == lax.broadcasted_iota(jnp.int32, (8, heads), 1)).astype(jnp.bfloat16)
    for tile in range(PEERS):
        allowed = lax.dot_general(
            pick,
            (mask_in[tile] > 0).astype(jnp.bfloat16),
            (((1,), (1,)), ((), ())),
            preferred_element_type=jnp.float32,
        )
        bias[tile, :, 0:PEERS] = jnp.where(allowed > 0.5, 0.0, NEGATIVE_FILL)

    exponent_scale = math.log2(math.e) / math.sqrt(dim)
    ones = jnp.ones((2 * dim, dim), jnp.bfloat16)
    step = 2 * dim

    def attend(slot, chip):
        rows = pl.ds(pl.multiple_of(chip * pair, pair), pair)
        biases = jnp.concatenate(
            [
                jnp.broadcast_to(bias[chip * CORES + i, slot : slot + 1, :], (tokens, dim))
                for i in range(CORES)
            ],
            axis=0,
        )
        queries = jnp.concatenate([qkv_got[slot, rows, 0:dim], biases.astype(jnp.bfloat16)], axis=1)
        largest = None
        for start in range(0, keys, step):
            part = slice(start, start + step)
            key_part = jnp.concatenate([qkv_got[slot, part, dim : 2 * dim], tile_of_key[part, :]], axis=1)
            found = lax.dot_general(
                queries, key_part, (((1,), (1,)), ((), ())), preferred_element_type=jnp.float32
            )
            scores[:, part] = found
            higher = jnp.maximum(found[:, 0:dim], found[:, dim:step])
            largest = higher if largest is None else jnp.maximum(largest, higher)
        row_max = jnp.max(largest, axis=1, keepdims=True)
        total = jnp.zeros((pair, 2 * dim), jnp.float32)
        for start in range(0, keys, step):
            part = slice(start, start + step)
            weights = jnp.exp2((scores[:, part] - row_max) * exponent_scale).astype(jnp.bfloat16)
            values = jnp.concatenate([qkv_got[slot, part, 2 * dim : 3 * dim], ones], axis=1)
            total += jnp.dot(weights, values, preferred_element_type=jnp.float32)
        o_out[slot, rows, :] = (total[:, 0:dim] / total[:, dim : 2 * dim]).astype(jnp.bfloat16)

    for slot in range(slots):
        own("qkv", slot).wait()
        all_of("qkv", slot).wait_recv()
        attend(slot, y)
        own("o", slot).start()
        remote("o", slot, 0, 1).start()

        def turn(number, carry, slot=slot):
            distance = (CHIPS - number) // 2
            d = jnp.where(number % 2 == 0, distance, CHIPS - distance)
            attend(slot, lax.rem(y + d, CHIPS))
            for f in range(CORES):
                remote("o", slot, d, f).start()
            return carry

        lax.fori_loop(0, CHIPS - 1, turn, 0)

    for slot in range(slots):
        all_of("qkv", slot).wait_send()
        own("o", slot).wait()
    all_of("o").wait_send()
    all_of("o").wait_recv()


def body(projections, tile_mask):
    tokens, heads, width = projections.shape
    dim = width // 3
    slots = heads // PEERS
    keys = tokens * PEERS
    return pl.pallas_call(
        kernel,
        out_shape=jax.ShapeDtypeStruct((tokens, heads * dim), jnp.bfloat16),
        in_specs=[pl.BlockSpec(memory_space=pltpu.HBM)] * 2,
        out_specs=pl.BlockSpec(memory_space=pl.ANY),
        scratch_shapes=[
            pltpu.VMEM((slots, tokens, PEERS, width), jnp.bfloat16),
            pltpu.VMEM((PEERS, PEERS, heads), jnp.int32),
            pltpu.VMEM((slots, PEERS, tokens, width), jnp.bfloat16),
            pltpu.VMEM((slots, keys, width), jnp.bfloat16),
            pltpu.VMEM((slots, keys, dim), jnp.bfloat16),
            pltpu.VMEM((keys, dim), jnp.bfloat16),
            pltpu.VMEM((PEERS, 8, dim), jnp.float32),
            pltpu.VMEM((CORES * tokens, keys), jnp.float32),
            pltpu.SemaphoreType.DMA((slots,)),
            pltpu.SemaphoreType.DMA,
            pltpu.SemaphoreType.DMA((2 * slots,)),
            pltpu.SemaphoreType.DMA((slots + 1,)),
            pltpu.SemaphoreType.DMA((slots + 1,)),
            pltpu.SemaphoreType.REGULAR,
        ],
        compiler_params=pltpu.CompilerParams(
            collective_id=0, has_side_effects=True, vmem_limit_bytes=48 << 20
        ),
    )(
        pltpu.with_memory_space_constraint(projections, pltpu.HBM),
        pltpu.with_memory_space_constraint(jnp.transpose(tile_mask, (1, 2, 0)), pltpu.HBM),
    )


def solution(mesh):
    return jax.shard_map(
        body,
        mesh=mesh,
        in_specs=(P(("clip", "seq", "tp"), None, None), P("clip", None, None)),
        out_specs=P(("clip", "seq", "tp"), None),
        check_vma=False,
    )
```

```python
import functools
import math

import jax
import jax.numpy as jnp
from jax import lax
from jax.experimental import pallas as pl
from jax.experimental.pallas import tpu as pltpu
from jax.sharding import PartitionSpec as P

MESH = pl.DeviceIdType.MESH
NEGATIVE_FILL = -1e30
CHIPS = 8
CORES = 2
PEERS = CHIPS * CORES
LATE = (0, 8, 9, 10, 11)
TELLS = ((1, 0), (6, 8), (7, 9), (12, 10), (13, 11))
REACH = (1, 7, 2, 6, 3, 5, 4)
SECOND = tuple((d, f) for d in (3, 5, 4, 2, 6, 1, 7) for f in range(CORES)) + ((0, 1),)
OFFSETS = tuple((d, f) for d in REACH for f in range(CORES)) + ((0, 1),)


def kernel(
    x_ref,
    mask_ref,
    out_ref,
    x_in,
    mask_in,
    qkv_out,
    qkv_got,
    o_out,
    tile_of_key,
    bias,
    scores,
    in_sem,
    mask_sem,
    own_sem,
    send_sem,
    recv_sem,
    ready_sem,
):
    y = lax.axis_index("seq")
    core = lax.axis_index("tp")
    me = y * CORES + core
    tokens, _, width = x_ref.shape
    slots = x_in.shape[0]
    dim = width // 3
    pair = CORES * tokens
    keys = qkv_got.shape[1]

    x_copies = [
        pltpu.make_async_copy(
            x_ref.at[:, pl.ds(slot * PEERS, PEERS), :], x_in.at[slot], in_sem.at[slot]
        )
        for slot in range(slots)
    ]
    x_copies[0].start()

    def peer(d, f):
        return {"seq": lax.rem(y + d, CHIPS), "tp": lax.rem(core + f, CORES)}

    def index_of(d, f):
        return lax.rem(y + d, CHIPS) * CORES + lax.rem(core + f, CORES)

    def is_late(device):
        return functools.reduce(jnp.logical_or, [device == late for late in LATE])

    barrier = pltpu.get_barrier_semaphore()
    late = is_late(me)
    early = jnp.logical_not(late)

    @pl.when(early)
    def _():
        for d, f in OFFSETS:
            pl.semaphore_signal(barrier, inc=1, device_id=peer(d, f), device_id_type=MESH)

    for copy in x_copies[1:]:
        copy.start()
    mask_copy = pltpu.make_async_copy(mask_ref, mask_in, mask_sem)
    mask_copy.start()

    @pl.when(late)
    def _():
        pl.semaphore_wait(barrier, PEERS - len(LATE))
        for d, f in OFFSETS:

            @pl.when(jnp.logical_not(is_late(index_of(d, f))))
            def _(d=d, f=f):
                pl.semaphore_signal(ready_sem, inc=1, device_id=peer(d, f), device_id_type=MESH)

    def rows_of(device):
        return pl.ds(pl.multiple_of(device * tokens, tokens), tokens)

    def ends(kind, slot, to):
        if kind == "qkv":
            return qkv_out.at[slot, to], qkv_got.at[slot, rows_of(me)], slot
        columns = pl.ds(pl.multiple_of((slot * PEERS + me) * dim, dim), dim)
        return o_out.at[slot, rows_of(to)], out_ref.at[:, columns], slots

    def remote(kind, slot, d, f):
        src, dst, number = ends(kind, slot, index_of(d, f))
        return pltpu.make_async_remote_copy(
            src_ref=src,
            dst_ref=dst,
            send_sem=send_sem.at[number],
            recv_sem=recv_sem.at[number],
            device_id=peer(d, f),
            device_id_type=MESH,
        )

    def all_of(kind, slot=0):
        others = PEERS - 1
        if kind == "qkv":
            src, dst, number = qkv_out.at[slot, 0:others], qkv_got.at[slot, 0 : others * tokens], slot
        else:
            src = o_out.at[:, 0 : others * tokens]
            dst, number = out_ref.at[:, 0 : slots * others * dim], slots
        return pltpu.make_async_remote_copy(
            src_ref=src,
            dst_ref=dst,
            send_sem=send_sem.at[number],
            recv_sem=recv_sem.at[number],
            device_id=peer(0, 1),
            device_id_type=MESH,
        )

    def own(kind, slot):
        src, dst, number = ends(kind, slot, me)
        return pltpu.make_async_copy(src, dst, own_sem.at[number + slot if kind == "o" else number])

    side = PEERS * PEERS
    to_row = lax.broadcasted_iota(jnp.int32, (side, side), 0)
    from_row = lax.broadcasted_iota(jnp.int32, (side, side), 1)
    swap = (from_row == (to_row % PEERS) * PEERS + to_row // PEERS).astype(jnp.bfloat16)

    def regroup(slot):
        for start in range(0, tokens, PEERS):
            block = x_in[slot, start : start + PEERS].reshape(side, width)
            swapped = jnp.dot(swap, block, preferred_element_type=jnp.float32)
            qkv_out[slot, :, start : start + PEERS, :] = swapped.astype(jnp.bfloat16).reshape(
                PEERS, PEERS, width
            )

    x_copies[0].wait()
    regroup(0)

    @pl.when(early)
    def _():
        pl.semaphore_wait(barrier, PEERS - len(LATE) - 1)

    for d, f in OFFSETS:

        @pl.when(jnp.logical_not(is_late(index_of(d, f))))
        def _(d=d, f=f):
            remote("qkv", 0, d, f).start()

    own("qkv", 0).start()
    x_copies[1].wait()
    regroup(1)

    @pl.when(early)
    def _():
        pl.semaphore_wait(ready_sem, len(LATE))
        for teller, told in TELLS:

            @pl.when(me == teller)
            def _(told=told):
                pl.semaphore_signal(
                    ready_sem,
                    inc=1,
                    device_id={"seq": told // CORES, "tp": told % CORES},
                    device_id_type=MESH,
                )

    @pl.when(late)
    def _():
        pl.semaphore_wait(ready_sem, 1)

    for d, f in OFFSETS:

        @pl.when(is_late(index_of(d, f)))
        def _(d=d, f=f):
            remote("qkv", 0, d, f).start()

    for d, f in SECOND:
        remote("qkv", 1, d, f).start()
    own("qkv", 1).start()

    tile_of_key[...] = (
        lax.broadcasted_iota(jnp.int32, tile_of_key.shape, 0) // tokens
        == lax.broadcasted_iota(jnp.int32, tile_of_key.shape, 1)
    ).astype(jnp.bfloat16)
    bias[...] = jnp.zeros_like(bias)
    mask_copy.wait()
    heads = mask_in.shape[2]
    my_head = lax.broadcasted_iota(jnp.int32, (8, heads), 0) * PEERS + me
    pick = (my_head == lax.broadcasted_iota(jnp.int32, (8, heads), 1)).astype(jnp.bfloat16)
    for tile in range(PEERS):
        allowed = lax.dot_general(
            pick,
            (mask_in[tile] > 0).astype(jnp.bfloat16),
            (((1,), (1,)), ((), ())),
            preferred_element_type=jnp.float32,
        )
        bias[tile, :, 0:PEERS] = jnp.where(allowed > 0.5, 0.0, NEGATIVE_FILL)

    exponent_scale = math.log2(math.e) / math.sqrt(dim)
    ones = jnp.ones((2 * dim, dim), jnp.bfloat16)
    step = 2 * dim

    def attend(slot, chip):
        rows = pl.ds(pl.multiple_of(chip * pair, pair), pair)
        biases = jnp.concatenate(
            [
                jnp.broadcast_to(bias[chip * CORES + i, slot : slot + 1, :], (tokens, dim))
                for i in range(CORES)
            ],
            axis=0,
        )
        queries = jnp.concatenate([qkv_got[slot, rows, 0:dim], biases.astype(jnp.bfloat16)], axis=1)
        largest = None
        for start in range(0, keys, step):
            part = slice(start, start + step)
            key_part = jnp.concatenate([qkv_got[slot, part, dim : 2 * dim], tile_of_key[part, :]], axis=1)
            found = lax.dot_general(
                queries, key_part, (((1,), (1,)), ((), ())), preferred_element_type=jnp.float32
            )
            scores[:, part] = found
            higher = jnp.maximum(found[:, 0:dim], found[:, dim:step])
            largest = higher if largest is None else jnp.maximum(largest, higher)
        row_max = jnp.max(largest, axis=1, keepdims=True)
        total = jnp.zeros((pair, 2 * dim), jnp.float32)
        for start in range(0, keys, step):
            part = slice(start, start + step)
            weights = jnp.exp2((scores[:, part] - row_max) * exponent_scale).astype(jnp.bfloat16)
            values = jnp.concatenate([qkv_got[slot, part, 2 * dim : 3 * dim], ones], axis=1)
            total += jnp.dot(weights, values, preferred_element_type=jnp.float32)
        o_out[slot, rows, :] = (total[:, 0:dim] / total[:, dim : 2 * dim]).astype(jnp.bfloat16)

    for slot in range(slots):
        own("qkv", slot).wait()
        all_of("qkv", slot).wait_recv()
        attend(slot, y)
        own("o", slot).start()
        remote("o", slot, 0, 1).start()

        def turn(number, carry, slot=slot):
            distance = (CHIPS - number) // 2
            d = jnp.where(number % 2 == 0, distance, CHIPS - distance)
            attend(slot, lax.rem(y + d, CHIPS))
            for f in range(CORES):
                remote("o", slot, d, f).start()
            return carry

        lax.fori_loop(0, CHIPS - 1, turn, 0)

    for slot in range(slots):
        all_of("qkv", slot).wait_send()
        own("o", slot).wait()
    all_of("o").wait_send()
    all_of("o").wait_recv()


def body(projections, tile_mask):
    tokens, heads, width = projections.shape
    dim = width // 3
    slots = heads // PEERS
    keys = tokens * PEERS
    return pl.pallas_call(
        kernel,
        out_shape=jax.ShapeDtypeStruct((tokens, heads * dim), jnp.bfloat16),
        in_specs=[pl.BlockSpec(memory_space=pltpu.HBM)] * 2,
        out_specs=pl.BlockSpec(memory_space=pl.ANY),
        scratch_shapes=[
            pltpu.VMEM((slots, tokens, PEERS, width), jnp.bfloat16),
            pltpu.VMEM((PEERS, PEERS, heads), jnp.int32),
            pltpu.VMEM((slots, PEERS, tokens, width), jnp.bfloat16),
            pltpu.VMEM((slots, keys, width), jnp.bfloat16),
            pltpu.VMEM((slots, keys, dim), jnp.bfloat16),
            pltpu.VMEM((keys, dim), jnp.bfloat16),
            pltpu.VMEM((PEERS, 8, dim), jnp.float32),
            pltpu.VMEM((CORES * tokens, keys), jnp.float32),
            pltpu.SemaphoreType.DMA((slots,)),
            pltpu.SemaphoreType.DMA,
            pltpu.SemaphoreType.DMA((2 * slots,)),
            pltpu.SemaphoreType.DMA((slots + 1,)),
            pltpu.SemaphoreType.DMA((slots + 1,)),
            pltpu.SemaphoreType.REGULAR,
        ],
        compiler_params=pltpu.CompilerParams(
            collective_id=0, has_side_effects=True, vmem_limit_bytes=48 << 20
        ),
    )(
        pltpu.with_memory_space_constraint(projections, pltpu.HBM),
        pltpu.with_memory_space_constraint(jnp.transpose(tile_mask, (1, 2, 0)), pltpu.HBM),
    )


def solution(mesh):
    return jax.shard_map(
        body,
        mesh=mesh,
        in_specs=(P(("clip", "seq", "tp"), None, None), P("clip", None, None)),
        out_specs=P(("clip", "seq", "tp"), None),
        check_vma=False,
    )
```
